256 devices in a mesh: dp: 16 (over y, z_lo, core), tensor: 16 (over z_hi, x).
Axes of the slice: x: 4, y: 4, z: 8 (z_hi: 4, z_lo: 2; z = z_hi * 2 + z_lo), core: 2. Of those that a mesh axis runs over, the one named last changes fastest.
Arguments:
- query: bfloat16 [6144, 8192], P('dp', 'tensor'), may hold values from -140 to 140
- keys: bfloat16 [6144, 1024], P('dp'), may hold values from -6 to 6
- values: bfloat16 [6144, 1024], P('dp'), may hold values from -6 to 6
- out_grad: bfloat16 [6144, 8192], P(('dp', 'tensor')), may hold values from -24 to 24
- lengths: int32 [48], replicated, may hold values from 1 to 128, 3840 in all
- order: int32 [48], replicated, may hold values from 0 to 47, each once
Outputs:
- importance: float32 [8192, 8192], P('dp', 'tensor')
The draws below stay inside these ranges and needn't reach their ends.
Inputs may be any that keep to these rules, and one draw needn't show every extreme that they name: `lengths`: the largest is exactly 128, and they sum to 3840. `order`: a permutation of the sequences over the slots.
All inputs are finite; a program needn't handle non-finite values.
Results may differ from the reference program's by a relative error of at most 0.0015.
Values may be sent and summed in bfloat16 or wider, within the bound.
A program may use at most 256 MiB of HBM per device.

```python
import math
import jax
import jax.numpy as jnp
import numpy as np
from jax import lax

D = 8192
HEADS = 64
KV_HEADS = 8
HEAD_DIM = 128
SLOT_LEN = 128
SLOTS = 3
HQ = 8192
KVD = 1024
SEQS = 48
TOKENS = 6144
N_DP = 16


def draw_keys(key, part):
    field = jnp.clip(jax.random.normal(key, (TOKENS, KVD), jnp.float32), -5.0, 5.0)
    return field.astype(jnp.bfloat16)


def draw_query(key, part):
    key = jax.random.fold_in(key, 3)
    drawn = jnp.clip(jax.random.normal(key, (TOKENS, HQ), jnp.float32), -5.0, 5.0)
    return drawn.astype(jnp.bfloat16)


def steps_of(rng, dims, cuts, least, top_value):
    def one(dim, shards_of):
        heights = jax.random.uniform(jax.random.fold_in(jax.random.fold_in(rng, 6), dim), (shards_of,), jnp.float32, least / len(cuts), top_value / len(cuts))
        return jnp.repeat(jnp.exp(heights), dims[dim] // shards_of).reshape((-1,) + (1,) * (len(dims) - dim - 1))

    level = one(*cuts[0])
    for cut in cuts[1:]:
        level = level * one(*cut)
    return level


def profile(count, total, reach, slope):
    weights = [(1 << 20) // math.isqrt(grade ** slope) + 1 for grade in range(2, count + 1)]
    spare, given = total - reach - (count - 1), [1] * (count - 1)
    while spare > 0:
        free = [i for i in range(count - 1) if given[i] < reach]
        mass, left = sum([weights[i] for i in free]), spare
        for i in free:
            addition = min(reach - given[i], max(1, left * weights[i] // mass), spare)
            given[i] = given[i] + addition
            spare = spare - addition
    return np.array([reach] + given)


def ragged(key, number_of, total, most, skew):
    if number_of == 2:
        one = jax.random.randint(key, (), max(1, total - most), min(most, total - 1) + 1)
        return jnp.stack([one, total - one])
    sizes = jnp.asarray(profile(number_of, total, most, skew), jnp.int32)
    twos = (number_of - 1) // 2
    donor, taker = sizes[1:1 + 2 * twos:2], sizes[2:2 + 2 * twos:2]
    margin = jnp.minimum(donor - 1, most - taker)
    moved = jax.random.randint(jax.random.fold_in(key, 1), (twos,), 0, 1 << 20) % (margin + 1)
    sizes = sizes.at[1:1 + 2 * twos:2].set(donor - moved).at[2:2 + 2 * twos:2].set(taker + moved)
    return sizes[jax.random.permutation(jax.random.fold_in(key, 2), number_of)]


def gaussian(own_key, extent, scale, bound, cuts=(), kind=jnp.bfloat16):
    loudness = steps_of(own_key, extent, cuts, -0.22, 0.18) if cuts else 1.0
    entries = jax.random.normal(own_key, extent, jnp.float32) * scale * loudness
    return jnp.minimum(jnp.maximum(entries, -bound), bound).astype(kind)


def setup_inputs(seed: int = 0) -> dict:
    arg_keys = jax.random.split(jax.random.key(seed), 7)
    return {
        "query": draw_query(jax.random.fold_in(arg_keys[6], 71), 0),
        "keys": draw_keys(jax.random.fold_in(arg_keys[6], 71), 0),
        "values": gaussian(arg_keys[2], (TOKENS, KVD), 1.0, 6.0, ((0, 16),)),
        "out_grad": gaussian(arg_keys[3], (TOKENS, D), 4.0, 24.0, ((0, 256),)),
        "lengths": ragged(arg_keys[4], SEQS, SEQS * SLOT_LEN * 5 // 8, SLOT_LEN, 1).astype(jnp.int32),
        "order": jax.random.permutation(arg_keys[5], SEQS).astype(jnp.int32),
    }


NEGATIVE_FILL = -1e+30

def attend(slot_query, slot_keys, slot_values, length):
    sharing = HEADS // KV_HEADS
    query_heads = slot_query.astype(jnp.float32).reshape(SLOT_LEN, HEADS, HEAD_DIM)
    key_heads = jnp.repeat(slot_keys.astype(jnp.float32).reshape(SLOT_LEN, KV_HEADS, HEAD_DIM), sharing, axis=1)
    value_heads = jnp.repeat(slot_values.astype(jnp.float32).reshape(SLOT_LEN, KV_HEADS, HEAD_DIM), sharing, axis=1)
    scores = jnp.einsum('qhd,khd->hqk', query_heads, key_heads) * (1.0 / math.sqrt(HEAD_DIM))
    row_index = jnp.arange(SLOT_LEN, dtype=jnp.int32)[:, None]
    col_index = jnp.arange(SLOT_LEN, dtype=jnp.int32)[None, :]
    allowed = (col_index <= row_index) & (col_index < length)
    scores = jnp.where(allowed[None], scores, NEGATIVE_FILL)
    peak = lax.optimization_barrier(jnp.max(scores, axis=2, keepdims=True))
    raised = jnp.exp(scores - peak)
    probs = (raised / lax.optimization_barrier(jnp.sum(raised, axis=2, keepdims=True))).astype(jnp.bfloat16)
    mixed = jnp.einsum('hqk,khd->qhd', probs.astype(jnp.float32), value_heads).reshape(SLOT_LEN, HQ)
    return jnp.where(row_index < length, mixed, 0.0).astype(jnp.bfloat16)

def reference(query, keys, values, out_grad, lengths, order):
    slot_lengths = jnp.take(lengths, order).reshape(N_DP, SLOTS)
    group_query = query.reshape(N_DP, SLOTS, SLOT_LEN, HQ)
    group_keys = keys.reshape(N_DP, SLOTS, SLOT_LEN, KVD)
    group_values = values.reshape(N_DP, SLOTS, SLOT_LEN, KVD)
    group_grad = out_grad.reshape(N_DP, SLOTS, SLOT_LEN, D)

    def add_group(running, inputs):
        one_query, one_keys, one_values, one_grad, one_lengths = inputs
        term = jnp.zeros((D, HQ), jnp.float32)
        for slot_pos in range(SLOTS):
            attention = attend(one_query[slot_pos], one_keys[slot_pos], one_values[slot_pos], one_lengths[slot_pos])
            gradient = lax.dot_general(one_grad[slot_pos], attention, (((0,), (0,)), ((), ())), preferred_element_type=jnp.float32)
            term = term + gradient * gradient
        return (running + term, None)
    summed, _ = lax.scan(add_group, jnp.zeros((D, HQ), jnp.float32), (group_query, group_keys, group_values, group_grad, slot_lengths))
    return summed * (1.0 / (SEQS * SLOT_LEN))
```

```python
import math

import jax
import jax.numpy as jnp
from jax import lax
from jax.experimental import pallas as pl
from jax.experimental.pallas import tpu as pltpu
from jax.sharding import PartitionSpec as P

HEADS = 64
KV_HEADS = 8
HEAD_DIM = 128
SLOT_LEN = 128
SLOTS = 3
NEGATIVE_FILL = -1e30

NX = 4
NZ = 4
NY = 4
GROUPS = 16
ROWS = SLOTS * SLOT_LEN
PIECE = 24
ZROWS = NX * PIECE
WIDTH = 128
FEATS = 512
CH = 2
NC = GROUPS // CH
MESH = pl.DeviceIdType.MESH


def kernel(
    lengths_ref, order_ref, q_ref, k_hbm, v_hbm, g_ref, out_ref,
    kbuf, vbuf, pk, r0, s1, gx, att, acc,
    kv_sem, x0_send, x0_recv, d_send, d_recv, z_send, z_recv, x_send, x_recv,
    a_send, a_recv, b_send, b_recv,
):
    d = lax.axis_index("dp")
    t = lax.axis_index("tensor")
    zh, x = t // NX, t % NX
    y, zl, c = d // 4, (d // 2) % 2, d % 2

    def at_x(step):
        return (x + step + NX) % NX

    def at_z(step):
        return (zh + step + NZ) % NZ

    def dp_of(dy, dz, dc):
        return ((y + dy) % NY) * 4 + ((zl + dz) % 2) * 2 + (c + dc) % 2

    def dev_x(step):
        return {"dp": d, "tensor": zh * NX + at_x(step)}

    def dev_z(step):
        return {"dp": d, "tensor": at_z(step) * NX + x}

    def dev_dp(dy, dz, dc):
        return {"dp": dp_of(dy, dz, dc), "tensor": t}

    def remote(src, dst, send, recv, device):
        return pltpu.make_async_remote_copy(
            src_ref=src, dst_ref=dst, send_sem=send, recv_sem=recv,
            device_id=device, device_id_type=MESH,
        )

    barrier = pltpu.get_barrier_semaphore()
    peers = [dev_x(s) for s in (1, 2, 3)] + [dev_z(1), dev_z(-1)]
    peers += [dev_dp(i // 4, (i // 2) % 2, i % 2) for i in range(1, GROUPS)]
    for peer in peers:
        pl.semaphore_signal(barrier, inc=1, device_id=peer, device_id_type=MESH)

    kv_cols = pl.ds(pl.multiple_of((t // 2) * HEAD_DIM, HEAD_DIM), HEAD_DIM)
    k_copy = pltpu.make_async_copy(k_hbm.at[:, kv_cols], kbuf, kv_sem.at[0])
    v_copy = pltpu.make_async_copy(v_hbm.at[:, kv_cols], vbuf, kv_sem.at[1])
    k_copy.start()
    v_copy.start()

    for xb in range(NX):
        for m in range(GROUPS // 2):
            parts = []
            for gg in (2 * m, 2 * m + 1):
                lo = (gg * NX + xb) * WIDTH
                parts.append(g_ref[:, lo : lo + WIDTH].astype(jnp.float32))
            both = jnp.concatenate(parts, axis=0)
            pk[xb, m * 2 * PIECE : (m + 1) * 2 * PIECE, :] = both.astype(jnp.bfloat16)

    pl.semaphore_wait(barrier, len(peers))

    sends = []

    def x0_copy(s):
        return remote(pk.at[at_x(s)], r0.at[x], x0_send.at[s - 1], x0_recv.at[s - 1], dev_x(s))

    for s in (1, 2, 3):
        x0_copy(s).start()
        sends.append(x0_copy(s))
    r0[x] = pk[x]

    k_copy.wait()
    v_copy.wait()
    key_index = lax.broadcasted_iota(jnp.int32, (SLOT_LEN, SLOT_LEN), 0)
    row_index = lax.broadcasted_iota(jnp.int32, (SLOT_LEN, SLOT_LEN), 1)
    scale = 1.0 / math.sqrt(HEAD_DIM)
    for s in range(SLOTS):
        length = lengths_ref[order_ref[d * SLOTS + s]]
        rows = slice(s * SLOT_LEN, (s + 1) * SLOT_LEN)
        allowed = (key_index <= row_index) & (key_index < length)
        live = row_index < length
        keys = kbuf[rows, :]
        values_t = vbuf[rows, :].astype(jnp.float32).T.astype(jnp.bfloat16)
        for h in range(FEATS // HEAD_DIM):
            feats = slice(h * HEAD_DIM, (h + 1) * HEAD_DIM)
            scores = lax.dot_general(
                keys, q_ref[rows, feats], (((1,), (1,)), ((), ())),
                preferred_element_type=jnp.float32,
            ) * scale
            scores = jnp.where(allowed, scores, NEGATIVE_FILL)
            peak = jnp.max(scores, axis=0, keepdims=True)
            raised = jnp.exp(scores - peak)
            probs = (raised / jnp.sum(raised, axis=0, keepdims=True)).astype(jnp.bfloat16)
            mixed = jnp.dot(values_t, probs, preferred_element_type=jnp.float32)
            att[0, feats, rows] = jnp.where(live, mixed, 0.0).astype(jnp.bfloat16)

    def a_copy(src, dst, n, dy, dz):
        return remote(att.at[2 * src], att.at[2 * dst], a_send.at[n], a_recv.at[dst], dev_dp(dy, dz, 0))

    def b_copy(q):
        return remote(att.at[2 * q], att.at[2 * q + 1], b_send.at[q], b_recv.at[q], dev_dp(0, 0, 1))

    def go(copy):
        copy.start()
        sends.append(copy)

    def a_wait(q):
        a_copy(q, q, 0, 0, 1).wait_recv()

    go(a_copy(0, 1, 0, 0, 1))
    go(a_copy(0, 6, 1, 1, 0))
    go(a_copy(0, 2, 2, 3, 0))
    go(b_copy(0))

    for s in (1, 2, 3):
        remote(pk.at[x], r0.at[at_x(-s)], x0_send.at[s - 1], x0_recv.at[s - 1], dev_x(s)).wait_recv()
    for m in range(GROUPS // 2):
        parts = [r0[xb, m * 2 * PIECE : (m + 1) * 2 * PIECE, :].astype(jnp.float32) for xb in range(NX)]
        for e in range(2):
            rows = jnp.concatenate([p[e * PIECE : (e + 1) * PIECE] for p in parts], axis=0)
            s1[2 * m + e] = rows.astype(jnp.bfloat16)

    own_rows = pl.ds(pl.multiple_of(zh * ZROWS, ZROWS), ZROWS)

    for i in range(1, GROUPS):
        dy, dz, dc = i // 4, (i // 2) % 2, i % 2
        j = ((NY - dy) % NY) * 4 + dz * 2 + dc
        go(remote(s1.at[dp_of(dy, dz, dc)], gx.at[x, j, own_rows], d_send.at[i], d_recv.at[j], dev_dp(dy, dz, dc)))
    gx[x, 0, own_rows, :] = s1[d]

    def z_piece(q, step):
        rows = pl.ds(pl.multiple_of(at_z(step) * ZROWS, ZROWS), ZROWS)
        return gx.at[x, pl.ds(q * CH, CH), rows]

    def z_copy(q, kind):
        if kind == 0:
            piece, step = z_piece(q, 0), 1
        elif kind == 1:
            piece, step = z_piece(q, 0), -1
        elif q % 2 == 0:
            piece, step = z_piece(q, -1), 1
        else:
            piece, step = z_piece(q, 1), -1
        return remote(piece, piece, z_send.at[kind, q], z_recv.at[kind, q], dev_z(step))

    def z_wait(q, kind):
        piece = z_piece(q, (-1, 1, 2)[kind])
        remote(piece, piece, z_send.at[kind, q], z_recv.at[kind, q], dev_z(1)).wait_recv()

    def x_piece(q, step):
        return gx.at[at_x(step), pl.ds(q * CH, CH)]

    def x_copy(q, kind):
        if kind == 0:
            piece, step = x_piece(q, 0), 1
        elif kind == 1:
            piece, step = x_piece(q, 0), -1
        elif q % 2 == 0:
            piece, step = x_piece(q, -1), 1
        else:
            piece, step = x_piece(q, 1), -1
        return remote(piece, piece, x_send.at[kind, q], x_recv.at[kind, q], dev_x(step))

    def x_wait(q, kind):
        piece = x_piece(q, (-1, 1, 2)[kind])
        remote(piece, piece, x_send.at[kind, q], x_recv.at[kind, q], dev_x(1)).wait_recv()

    def add_block(xb, i):
        total = None
        for s in range(SLOTS):
            rows = slice(s * SLOT_LEN, (s + 1) * SLOT_LEN)
            gradient = jnp.dot(att[i, :, rows], gx[xb, i, rows, :], preferred_element_type=jnp.float32)
            square = gradient * gradient
            total = square if total is None else total + square
        acc[xb] += total

    def add_blocks(q, first, count):
        def body(n, carry):
            add_block((x + first + n // CH) % NX, q * CH + n % CH)
            return carry

        lax.fori_loop(0, count * CH, body, 0)

    def z_own(q):
        if q == 0:
            d_wait(1)
        else:
            for i in range(q * CH, (q + 1) * CH):
                d_wait(i)
        go(z_copy(q, 0))
        go(z_copy(q, 1))

    def d_wait(i):
        remote(s1.at[0], gx.at[x, i, own_rows], d_send.at[i], d_recv.at[i], dev_dp(0, 0, 1)).wait_recv()

    acc[...] = jnp.zeros_like(acc)
    z_own(0)
    z_own(1)
    a_events = {
        0: [1],
        1: [6, 3],
        2: [2, 7],
        3: [4],
        4: [5],
    }

    def a_event(q):
        a_wait(q)
        if q == 1:
            go(a_copy(1, 7, 3, 1, 0))
            go(a_copy(1, 3, 4, 3, 0))
        if q == 6:
            go(a_copy(6, 4, 5, 1, 0))
        if q == 3:
            go(a_copy(3, 5, 6, 3, 0))
        go(b_copy(q))

    for n in range(NC + 3):
        if n < NC:
            z_wait(n, 0)
            z_wait(n, 1)
            go(z_copy(n, 2))
            if n + 2 < NC:
                z_own(n + 2)
        if 0 <= n - 1 < NC:
            z_wait(n - 1, 2)
            go(x_copy(n - 1, 0))
            go(x_copy(n - 1, 1))
        for q in a_events.get(n, ()):
            a_event(q)
        if 0 <= n - 2 < NC:
            x_wait(n - 2, 0)
            x_wait(n - 2, 1)
            go(x_copy(n - 2, 2))
            b_copy(n - 2).wait_recv()
            add_blocks(n - 2, 3, 3)
        if 0 <= n - 3 < NC:
            x_wait(n - 3, 2)
            add_blocks(n - 3, 2, 1)

    for xb in range(NX):
        out_ref[xb * WIDTH : (xb + 1) * WIDTH, :] = acc[xb].T

    for copy in sends:
        copy.wait_send()


def local(query, keys, values, out_grad, lengths, order):
    vmem = pl.BlockSpec(memory_space=pltpu.VMEM)
    smem = pl.BlockSpec(memory_space=pltpu.SMEM)
    hbm = pl.BlockSpec(memory_space=pl.ANY)
    bf16 = jnp.bfloat16
    dma = pltpu.SemaphoreType.DMA
    summed = pl.pallas_call(
        kernel,
        out_shape=jax.ShapeDtypeStruct((NX * WIDTH, FEATS), jnp.float32),
        in_specs=[smem, smem, vmem, hbm, hbm, vmem],
        out_specs=vmem,
        scratch_shapes=[
            pltpu.VMEM((ROWS, HEAD_DIM), bf16),
            pltpu.VMEM((ROWS, HEAD_DIM), bf16),
            pltpu.VMEM((NX, GROUPS * PIECE, WIDTH), bf16),
            pltpu.VMEM((NX, GROUPS * PIECE, WIDTH), bf16),
            pltpu.VMEM((GROUPS, ZROWS, WIDTH), bf16),
            pltpu.VMEM((NX, GROUPS, ROWS, WIDTH), bf16),
            pltpu.VMEM((GROUPS, FEATS, ROWS), bf16),
            pltpu.VMEM((NX, FEATS, WIDTH), jnp.float32),
            dma((2,)),
            dma((3,)), dma((3,)),
            dma((GROUPS,)), dma((GROUPS,)),
            dma((3, NC)), dma((3, NC)),
            dma((3, NC)), dma((3, NC)),
            dma((8,)), dma((8,)),
            dma((8,)), dma((8,)),
        ],
        compiler_params=pltpu.CompilerParams(
            collective_id=0, has_side_effects=True, vmem_limit_bytes=44 * 1024 * 1024
        ),
        cost_estimate=pl.CostEstimate(
            flops=2 * 48 * 128 * 512 * 512, bytes_accessed=4 * 1024 * 1024, transcendentals=12 * 128 * 128
        ),
    )(lengths, order, query, keys, values, out_grad)
    return summed * (1.0 / (GROUPS * ROWS))


def solution(mesh):
    placed = (P("dp", "tensor"), P("dp", None), P("dp", None), P(("dp", "tensor"), None), P(), P())
    return jax.shard_map(
        local, mesh=mesh, in_specs=placed, out_specs=P("dp", "tensor"), check_vma=False
    )
```

```python
import math

import jax
import jax.numpy as jnp
from jax import lax
from jax.experimental import pallas as pl
from jax.experimental.pallas import tpu as pltpu
from jax.sharding import PartitionSpec as P

HEADS = 64
KV_HEADS = 8
HEAD_DIM = 128
SLOT_LEN = 128
SLOTS = 3
NEGATIVE_FILL = -1e30

NX = 4
NZ = 4
NY = 4
GROUPS = 16
ROWS = SLOTS * SLOT_LEN
PIECE = 24
ZROWS = NX * PIECE
WIDTH = 128
FEATS = 512
PARTS = (0, 2, 1, 3)
X_FIRST = (0, 1, 2)
DIRECT = (3, 4, 5, 6)
ORDER = (
    ("xo", 0), ("xo", 1), ("xo", 2), ("zo", 3), ("zo", 8), ("zo", 12), ("zo", 4), ("xp", 0),
    ("zo", 9), ("zo", 5), ("xp", 1), ("xp", 2), ("zo", 6), ("zp", 8), ("zo", 7), ("xo", 3),
    ("zp", 12), ("zo", 10), ("A", 0), ("zp", 9), ("zo", 11), ("xo", 4), ("xp", 3), ("xo", 5),
    ("xo", 8), ("xp", 4), ("xo", 6), ("zp", 7), ("zo", 13), ("zp", 10), ("zo", 14), ("xp", 5),
    ("xo", 12), ("A", 2), ("A", 6), ("c3", 4), ("c3", 5), ("xp", 8), ("c1", 4), ("xp", 6),
    ("c1", 5), ("A", 1), ("c3", 3), ("xp", 12), ("xo", 9), ("zp", 11), ("zo", 15), ("c1", 3),
    ("xo", 7), ("A", 4), ("c3", 8), ("zp", 13), ("zo", 0), ("c1", 8), ("xo", 10), ("c3", 12),
    ("zp", 14), ("zo", 1), ("c1", 12), ("zp", 15), ("xp", 9), ("xo", 11), ("zo", 2), ("c3", 9),
    ("xp", 7), ("xo", 13), ("A", 3), ("A", 7), ("c3", 6), ("c1", 6), ("xp", 10), ("c3", 7),
    ("zp", 0), ("xo", 14), ("c1", 9), ("xp", 11), ("c1", 7), ("zp", 1), ("xo", 15), ("xp", 13),
    ("c3", 13), ("A", 5), ("c3", 10), ("c1", 10), ("c3", 11), ("zp", 2), ("xp", 14), ("c3", 14),
    ("c1", 11), ("c4", 0), ("xp", 15), ("c3", 15), ("c1", 13), ("c1", 14), ("c4", 1), ("c4", 2),
    ("c1", 15),
)
MESH = pl.DeviceIdType.MESH


def kernel(
    lengths_hbm, order_hbm, q_hbm, k_hbm, v_hbm, g_hbm, out_ref,
    lengths_ref, order_ref, q_ref, g_ref, kbuf, vbuf, pk, r0, s1, gx, att, acc,
    kv_sem, x0_send, x0_recv, d_send, d_recv, z_send, z_recv, x_send, x_recv,
    a_send, a_recv, b_send, b_recv,
):
    d = lax.axis_index("dp")
    t = lax.axis_index("tensor")
    zh, x = t // NX, t % NX
    y, zl, c = d // 4, (d // 2) % 2, d % 2

    def at_x(step):
        return (x + step + NX) % NX

    def at_z(step):
        return (zh + step + NZ) % NZ

    def dp_of(dy, dz, dc):
        return ((y + dy) % NY) * 4 + ((zl + dz) % 2) * 2 + (c + dc) % 2

    def dev_x(step):
        return {"dp": d, "tensor": zh * NX + at_x(step)}

    def dev_z(step):
        return {"dp": d, "tensor": at_z(step) * NX + x}

    def dev_dp(dy, dz, dc):
        return {"dp": dp_of(dy, dz, dc), "tensor": t}

    def remote(src, dst, send, recv, device):
        return pltpu.make_async_remote_copy(
            src_ref=src, dst_ref=dst, send_sem=send, recv_sem=recv,
            device_id=device, device_id_type=MESH,
        )

    barrier = pltpu.get_barrier_semaphore()
    peers = [dev_x(s) for s in (1, 2, 3)] + [dev_z(s) for s in (1, 2, 3)]
    peers += [dev_dp(i // 4, (i // 2) % 2, i % 2) for i in range(1, GROUPS)]
    for peer in peers:
        pl.semaphore_signal(barrier, inc=1, device_id=peer, device_id_type=MESH)

    g_copy = pltpu.make_async_copy(g_hbm, g_ref, kv_sem.at[2])
    q_copy = pltpu.make_async_copy(q_hbm, q_ref, kv_sem.at[3])
    l_copy = pltpu.make_async_copy(lengths_hbm, lengths_ref, kv_sem.at[4])
    o_copy = pltpu.make_async_copy(order_hbm, order_ref, kv_sem.at[5])
    g_copy.start()
    kv_cols = pl.ds(pl.multiple_of((t // 2) * HEAD_DIM, HEAD_DIM), HEAD_DIM)
    k_copy = pltpu.make_async_copy(k_hbm.at[:, kv_cols], kbuf, kv_sem.at[0])
    v_copy = pltpu.make_async_copy(v_hbm.at[:, kv_cols], vbuf, kv_sem.at[1])
    k_copy.start()
    q_copy.start()
    v_copy.start()
    l_copy.start()
    o_copy.start()
    g_copy.wait()

    for i in range(0, GROUPS, 2):
        lanes = [dp_of(j // 4, (j // 2) % 2, j % 2) * FEATS for j in (i, i + 1)]
        for xb in range(NX):
            parts = []
            for lane in lanes:
                cols = pl.ds(pl.multiple_of(lane + xb * WIDTH, WIDTH), WIDTH)
                parts.append(g_ref[:, cols].astype(jnp.float32))
            both = jnp.concatenate(parts, axis=0)
            pk[xb, i * PIECE : (i + 2) * PIECE, :] = both.astype(jnp.bfloat16)

    pl.semaphore_wait(barrier, len(peers))

    sends = []

    def go(copy):
        copy.start()
        sends.append(copy)

    def x0_rows(dy):
        return pl.ds(dy * 4 * PIECE, 4 * PIECE)

    for dy in PARTS:
        for s in (1, 2, 3):
            go(remote(
                pk.at[at_x(s), x0_rows(dy)], r0.at[x, x0_rows(dy)],
                x0_send.at[s - 1, dy], x0_recv.at[s - 1, dy], dev_x(s),
            ))
    r0[x] = pk[x]
    acc[...] = jnp.zeros_like(acc)

    k_copy.wait()
    v_copy.wait()
    q_copy.wait()
    l_copy.wait()
    o_copy.wait()
    key_index = lax.broadcasted_iota(jnp.int32, (SLOT_LEN, SLOT_LEN), 0)
    row_index = lax.broadcasted_iota(jnp.int32, (SLOT_LEN, SLOT_LEN), 1)
    scale = 1.0 / math.sqrt(HEAD_DIM)
    for s in range(SLOTS):
        length = lengths_ref[order_ref[d * SLOTS + s]]
        rows = slice(s * SLOT_LEN, (s + 1) * SLOT_LEN)
        allowed = (key_index <= row_index) & (key_index < length)
        live = row_index < length
        keys = kbuf[rows, :]
        values_t = vbuf[rows, :].astype(jnp.float32).T.astype(jnp.bfloat16)
        for h in range(FEATS // HEAD_DIM):
            feats = slice(h * HEAD_DIM, (h + 1) * HEAD_DIM)
            scores = lax.dot_general(
                keys, q_ref[rows, feats], (((1,), (1,)), ((), ())),
                preferred_element_type=jnp.float32,
            ) * scale
            scores = jnp.where(allowed, scores, NEGATIVE_FILL)
            peak = jnp.max(scores, axis=0, keepdims=True)
            raised = jnp.exp(scores - peak)
            probs = (raised / jnp.sum(raised, axis=0, keepdims=True)).astype(jnp.bfloat16)
            mixed = jnp.dot(values_t, probs, preferred_element_type=jnp.float32)
            att[0, feats, rows] = jnp.where(live, mixed, 0.0).astype(jnp.bfloat16)

    def a_copy(src, dst, n, dy, dz):
        return remote(att.at[2 * src], att.at[2 * dst], a_send.at[n], a_recv.at[dst], dev_dp(dy, dz, 0))

    def b_copy(q):
        return remote(att.at[2 * q], att.at[2 * q + 1], b_send.at[q], b_recv.at[q], dev_dp(0, 0, 1))

    def a_wait(q):
        a_copy(q, q, 0, 0, 1).wait_recv()

    own_rows = pl.ds(pl.multiple_of(zh * ZROWS, ZROWS), ZROWS)

    for dy in PARTS:
        for s in (1, 2, 3):
            remote(
                pk.at[x, x0_rows(dy)], r0.at[at_x(-s), x0_rows(dy)],
                x0_send.at[s - 1, dy], x0_recv.at[s - 1, dy], dev_x(s),
            ).wait_recv()
        for i in range(dy * 4, dy * 4 + 4, 2):
            parts = [r0[xb, i * PIECE : (i + 2) * PIECE, :].astype(jnp.float32) for xb in range(NX)]
            for e in range(2):
                rows = jnp.concatenate([p[e * PIECE : (e + 1) * PIECE] for p in parts], axis=0)
                s1[i + e] = rows.astype(jnp.bfloat16)
        for i in range(dy * 4, dy * 4 + 4):
            if i == 0:
                gx[x, 0, own_rows, :] = s1[0]
                continue
            dz, dc = (i // 2) % 2, i % 2
            j = ((NY - dy) % NY) * 4 + dz * 2 + dc
            go(remote(s1.at[i], gx.at[x, j, own_rows], d_send.at[i], d_recv.at[j], dev_dp(dy, dz, dc)))

    def d_wait(i):
        remote(s1.at[i], gx.at[x, i, own_rows], d_send.at[i], d_recv.at[i], dev_dp(0, 0, 1)).wait_recv()

    def rows_of(start, size, kind):
        if kind < 2:
            return pl.ds(pl.multiple_of(start, 16), size)
        return pl.ds(pl.multiple_of(start + (kind - 2) * (size // 2), 16), size // 2)

    def z_piece(i, step, kind):
        if i in DIRECT:
            kind = 0
        rows = rows_of(at_z(step) * ZROWS, ZROWS, kind)
        return gx.at[:, i, rows] if i in X_FIRST else gx.at[x, i, rows]

    def x_piece(i, step, kind):
        rows = rows_of(zh * ZROWS, ZROWS, kind) if i in X_FIRST else rows_of(0, ROWS, kind)
        return gx.at[at_x(step), i, rows]

    def z_ring(i, kind, arriving):
        if i in DIRECT:
            held = (-1, 1, 2)[kind] if arriving else 0
            step = (1, -1, 2)[kind]
        else:
            held = (-1, 1, 2, 2)[kind] if arriving else (0, 0, -1, 1)[kind]
            step = (1, -1, 1, -1)[kind]
        part = z_piece(i, held, kind)
        return remote(part, part, z_send.at[kind, i], z_recv.at[kind, i], dev_z(step))

    def x_ring(i, kind, arriving):
        held = (-1, 1, 2, 2)[kind] if arriving else (0, 0, -1, 1)[kind]
        step = (1, -1, 1, -1)[kind]
        part = x_piece(i, held, kind)
        return remote(part, part, x_send.at[kind, i], x_recv.at[kind, i], dev_x(step))

    def add_block(xb, i):
        total = None
        for s in range(SLOTS):
            rows = slice(s * SLOT_LEN, (s + 1) * SLOT_LEN)
            gradient = jnp.dot(att[i, :, rows], gx[xb, i, rows, :], preferred_element_type=jnp.float32)
            square = gradient * gradient
            total = square if total is None else total + square
        acc[xb] += total

    def add_blocks(i, first, count):
        def body(n, carry):
            add_block((x + first + n) % NX, i)
            return carry

        lax.fori_loop(0, count, body, 0)

    waited = set()

    def need(kind, *at):
        if (kind, at) in waited:
            return
        waited.add((kind, at))
        if kind == "d":
            d_wait(*at)
        elif kind == "z":
            z_ring(*at, True).wait_recv()
        elif kind == "x":
            x_ring(*at, True).wait_recv()
        elif kind == "a":
            a_wait(*at)
        else:
            b_copy(*at).wait_recv()

    def need_z(i):
        for kind in range(3 if i in DIRECT else 4):
            need("z", i, kind)

    def need_d(i):
        if i > 0:
            need("d", i)

    def step(kind, i):
        if kind == "A":
            if i == 0:
                go(a_copy(0, 1, 0, 0, 1))
                go(a_copy(0, 6, 1, 1, 0))
                go(a_copy(0, 2, 2, 3, 0))
                go(a_copy(0, 4, 6, 2, 0))
            else:
                need("a", i)
            if i == 1:
                go(a_copy(1, 7, 3, 1, 0))
                go(a_copy(1, 3, 4, 3, 0))
                go(a_copy(1, 5, 5, 2, 0))
            go(b_copy(i))
        elif kind == "zo":
            if i in X_FIRST:
                for part in range(4):
                    need("x", i, part)
            else:
                need_d(i)
            for part in range(3 if i in DIRECT else 2):
                go(z_ring(i, part, False))
        elif kind == "zp":
            for part in range(2):
                need("z", i, part)
            for part in (2, 3):
                go(z_ring(i, part, False))
        elif kind == "xo":
            if i in X_FIRST:
                need_d(i)
            else:
                need_z(i)
            for part in range(2):
                go(x_ring(i, part, False))
        elif kind == "xp":
            for part in range(2):
                need("x", i, part)
            for part in (2, 3):
                go(x_ring(i, part, False))
        else:
            if i % 2:
                need("b", i // 2)
            if kind == "c4":
                need_z(i)
                add_blocks(i, 0, 4)
            elif kind == "c3":
                need("x", i, 0)
                need("x", i, 1)
                add_blocks(i, 3, 3)
            else:
                need("x", i, 2)
                need("x", i, 3)
                add_blocks(i, 2, 1)

    for kind, i in ORDER:
        step(kind, i)

    for xb in range(NX):
        out_ref[xb * WIDTH : (xb + 1) * WIDTH, :] = acc[xb].T * (1.0 / (GROUPS * ROWS))

    for copy in sends:
        copy.wait_send()


def local(query, keys, values, out_grad, lengths, order):
    vmem = pl.BlockSpec(memory_space=pltpu.VMEM)
    hbm = pl.BlockSpec(memory_space=pl.ANY)
    bf16 = jnp.bfloat16
    dma = pltpu.SemaphoreType.DMA
    summed = pl.pallas_call(
        kernel,
        out_shape=jax.ShapeDtypeStruct((NX * WIDTH, FEATS), jnp.float32),
        in_specs=[hbm] * 6,
        out_specs=vmem,
        scratch_shapes=[
            pltpu.SMEM(lengths.shape, jnp.int32),
            pltpu.SMEM(order.shape, jnp.int32),
            pltpu.VMEM(query.shape, bf16),
            pltpu.VMEM(out_grad.shape, bf16),
            pltpu.VMEM((ROWS, HEAD_DIM), bf16),
            pltpu.VMEM((ROWS, HEAD_DIM), bf16),
            pltpu.VMEM((NX, GROUPS * PIECE, WIDTH), bf16),
            pltpu.VMEM((NX, GROUPS * PIECE, WIDTH), bf16),
            pltpu.VMEM((GROUPS, ZROWS, WIDTH), bf16),
            pltpu.VMEM((NX, GROUPS, ROWS, WIDTH), bf16),
            pltpu.VMEM((GROUPS, FEATS, ROWS), bf16),
            pltpu.VMEM((NX, FEATS, WIDTH), jnp.float32),
            dma((6,)),
            dma((3, NY)), dma((3, NY)),
            dma((GROUPS,)), dma((GROUPS,)),
            dma((4, GROUPS)), dma((4, GROUPS)),
            dma((4, GROUPS)), dma((4, GROUPS)),
            dma((8,)), dma((8,)),
            dma((8,)), dma((8,)),
        ],
        compiler_params=pltpu.CompilerParams(
            collective_id=0, has_side_effects=True, vmem_limit_bytes=60 * 1024 * 1024
        ),
        cost_estimate=pl.CostEstimate(
            flops=2 * 48 * 128 * 512 * 512, bytes_accessed=4 * 1024 * 1024, transcendentals=12 * 128 * 128
        ),
    )(lengths, order, query, keys, values, out_grad)
    return summed


def solution(mesh):
    placed = (P("dp", "tensor"), P("dp", None), P("dp", None), P(("dp", "tensor"), None), P(), P())
    return jax.shard_map(
        local, mesh=mesh, in_specs=placed, out_specs=P("dp", "tensor"), check_vma=False
    )
```

```python
import math

import jax
import jax.numpy as jnp
from jax import lax
from jax.experimental import pallas as pl
from jax.experimental.pallas import tpu as pltpu
from jax.sharding import PartitionSpec as P

HEADS = 64
KV_HEADS = 8
HEAD_DIM = 128
SLOT_LEN = 128
SLOTS = 3
NEGATIVE_FILL = -1e30

NX = 4
NZ = 4
NY = 4
GROUPS = 16
ROWS = SLOTS * SLOT_LEN
PIECE = 24
ZROWS = NX * PIECE
WIDTH = 128
FEATS = 512
PARTS = (0, 2, 1, 3)
X_FIRST = (0, 1, 2, 3)
DIRECT = ()
ORDER = (
    ("T", 0), ("T", 1), ("T", 2), ("P", 0), ("P", 2), ("P", 1), ("P", 3), ("xo", 0),
    ("xo", 1), ("xo", 2), ("xo", 3), ("zo", 8), ("zo", 12), ("zo", 4), ("xp", 0), ("zo", 9),
    ("xp", 1), ("xp", 2), ("xp", 3), ("zp", 8), ("zo", 5), ("zp", 12), ("zo", 6), ("Az", 0),
    ("Ay", 0), ("Ao", 0), ("A", 0), ("zp", 4), ("zo", 7), ("zp", 9), ("zo", 10), ("xo", 8),
    ("zp", 5), ("zo", 11), ("xo", 12), ("zp", 6), ("zo", 13), ("xp", 8), ("xp", 12), ("A", 2),
    ("A", 6), ("c3", 12), ("Ay", 1), ("Ao", 1), ("A", 1), ("c1", 12), ("xo", 4), ("zp", 7),
    ("zo", 14), ("xo", 9), ("zp", 10), ("zo", 15), ("xo", 5), ("zp", 11), ("zo", 0), ("xp", 4),
    ("xo", 6), ("c3", 4), ("zp", 13), ("zo", 1), ("A", 4), ("c3", 8), ("xp", 9), ("zp", 14),
    ("xo", 7), ("zo", 2), ("c1", 8), ("c3", 9), ("xp", 5), ("zp", 15), ("xo", 10), ("zo", 3),
    ("c3", 5), ("c1", 4), ("xp", 6), ("xo", 11), ("c1", 9), ("zp", 0), ("A", 3), ("A", 7),
    ("c3", 6), ("xp", 7), ("xo", 13), ("c3", 7), ("c1", 5), ("zp", 1), ("xp", 10), ("xo", 14),
    ("c1", 6), ("xp", 11), ("c1", 7), ("A", 5), ("c3", 10), ("zp", 2), ("xo", 15), ("c3", 11),
    ("xp", 13), ("c3", 13), ("c1", 10), ("zp", 3), ("xp", 14), ("c3", 14), ("c1", 11), ("c4", 0),
    ("xp", 15), ("c3", 15), ("c1", 13), ("c4", 1), ("c1", 14), ("c4", 2), ("c1", 15), ("c4", 3),
)
MESH = pl.DeviceIdType.MESH


def kernel(
    lengths_hbm, order_hbm, q_hbm, k_hbm, v_hbm, g_hbm, out_ref,
    lengths_ref, order_ref, q_ref, g_ref, kbuf, vbuf, pk, r0, s1, gx, att, acc,
    kv_sem, x0_send, x0_recv, d_send, d_recv, z_send, z_recv, x_send, x_recv,
    a_send, a_recv, b_send, b_recv,
):
    d = lax.axis_index("dp")
    t = lax.axis_index("tensor")
    zh, x = t // NX, t % NX
    y, zl, c = d // 4, (d // 2) % 2, d % 2

    def at_x(step):
        return (x + step + NX) % NX

    def at_z(step):
        return (zh + step + NZ) % NZ

    def dp_of(dy, dz, dc):
        return ((y + dy) % NY) * 4 + ((zl + dz) % 2) * 2 + (c + dc) % 2

    def dev_x(step):
        return {"dp": d, "tensor": zh * NX + at_x(step)}

    def dev_z(step):
        return {"dp": d, "tensor": at_z(step) * NX + x}

    def dev_dp(dy, dz, dc):
        return {"dp": dp_of(dy, dz, dc), "tensor": t}

    def remote(src, dst, send, recv, device):
        return pltpu.make_async_remote_copy(
            src_ref=src, dst_ref=dst, send_sem=send, recv_sem=recv,
            device_id=device, device_id_type=MESH,
        )

    barrier = pltpu.get_barrier_semaphore()
    peers = [dev_x(s) for s in (1, 2, 3)] + [dev_z(s) for s in (1, 2, 3)]
    peers += [dev_dp(i // 4, (i // 2) % 2, i % 2) for i in range(1, GROUPS)]
    for peer in peers:
        pl.semaphore_signal(barrier, inc=1, device_id=peer, device_id_type=MESH)

    g_copy = pltpu.make_async_copy(g_hbm, g_ref, kv_sem.at[2])
    q_copy = pltpu.make_async_copy(q_hbm, q_ref, kv_sem.at[3])
    l_copy = pltpu.make_async_copy(lengths_hbm, lengths_ref, kv_sem.at[4])
    o_copy = pltpu.make_async_copy(order_hbm, order_ref, kv_sem.at[5])
    g_copy.start()
    kv_cols = pl.ds(pl.multiple_of((t // 2) * HEAD_DIM, HEAD_DIM), HEAD_DIM)
    k_copy = pltpu.make_async_copy(k_hbm.at[:, kv_cols], kbuf, kv_sem.at[0])
    v_copy = pltpu.make_async_copy(v_hbm.at[:, kv_cols], vbuf, kv_sem.at[1])
    k_copy.start()
    q_copy.start()
    v_copy.start()
    l_copy.start()
    o_copy.start()
    g_copy.wait()

    for i in range(0, GROUPS, 2):
        lanes = [dp_of(j // 4, (j // 2) % 2, j % 2) * FEATS for j in (i, i + 1)]
        for xb in range(NX):
            parts = []
            for lane in lanes:
                cols = pl.ds(pl.multiple_of(lane + xb * WIDTH, WIDTH), WIDTH)
                parts.append(g_ref[:, cols].astype(jnp.float32))
            both = jnp.concatenate(parts, axis=0)
            pk[xb, i * PIECE : (i + 2) * PIECE, :] = both.astype(jnp.bfloat16)

    pl.semaphore_wait(barrier, len(peers))

    def go(copy):
        copy.start()

    def x0_rows(dy):
        return pl.ds(dy * 4 * PIECE, 4 * PIECE)

    def x0_start(dy):
        for s in (1, 2, 3):
            go(remote(
                pk.at[at_x(s), x0_rows(dy)], r0.at[x, x0_rows(dy)],
                x0_send, x0_recv.at[s - 1, dy], dev_x(s),
            ))

    for dy in PARTS:
        x0_start(dy)
    r0[x] = pk[x]
    acc[...] = jnp.zeros_like(acc)
    k_copy.wait()
    v_copy.wait()
    q_copy.wait()
    l_copy.wait()
    o_copy.wait()

    key_index = lax.broadcasted_iota(jnp.int32, (SLOT_LEN, SLOT_LEN), 0)
    row_index = lax.broadcasted_iota(jnp.int32, (SLOT_LEN, SLOT_LEN), 1)
    scale = 1.0 / math.sqrt(HEAD_DIM)
    def attend(s):
        length = lengths_ref[order_ref[d * SLOTS + s]]
        rows = slice(s * SLOT_LEN, (s + 1) * SLOT_LEN)
        allowed = (key_index <= row_index) & (key_index < length)
        live = row_index < length
        keys = kbuf[rows, :]
        values_t = vbuf[rows, :].astype(jnp.float32).T.astype(jnp.bfloat16)
        for h in range(FEATS // HEAD_DIM):
            feats = slice(h * HEAD_DIM, (h + 1) * HEAD_DIM)
            scores = lax.dot_general(
                keys, q_ref[rows, feats], (((1,), (1,)), ((), ())),
                preferred_element_type=jnp.float32,
            ) * scale
            scores = jnp.where(allowed, scores, NEGATIVE_FILL)
            peak = jnp.max(scores, axis=0, keepdims=True)
            raised = jnp.exp(scores - peak)
            probs = (raised / jnp.sum(raised, axis=0, keepdims=True)).astype(jnp.bfloat16)
            mixed = jnp.dot(values_t, probs, preferred_element_type=jnp.float32)
            att[0, feats, rows] = jnp.where(live, mixed, 0.0).astype(jnp.bfloat16)

    def a_copy(src, dst, n, dy, dz):
        return remote(att.at[2 * src], att.at[2 * dst], a_send, a_recv.at[dst], dev_dp(dy, dz, 0))

    def b_copy(q):
        return remote(att.at[2 * q], att.at[2 * q + 1], b_send, b_recv.at[q], dev_dp(0, 0, 1))

    def a_wait(q):
        a_copy(q, q, 0, 0, 1).wait_recv()

    own_rows = pl.ds(pl.multiple_of(zh * ZROWS, ZROWS), ZROWS)

    def dp_part(dy):
        for s in (1, 2, 3):
            remote(
                pk.at[x, x0_rows(dy)], r0.at[at_x(-s), x0_rows(dy)],
                x0_send, x0_recv.at[s - 1, dy], dev_x(s),
            ).wait_recv()
        for i in range(dy * 4, dy * 4 + 4, 2):
            parts = [r0[xb, i * PIECE : (i + 2) * PIECE, :].astype(jnp.float32) for xb in range(NX)]
            for e in range(2):
                rows = jnp.concatenate([p[e * PIECE : (e + 1) * PIECE] for p in parts], axis=0)
                s1[i + e] = rows.astype(jnp.bfloat16)
        for i in range(dy * 4, dy * 4 + 4):
            if i == 0:
                gx[x, 0, own_rows, :] = s1[0]
                continue
            dz, dc = (i // 2) % 2, i % 2
            j = ((NY - dy) % NY) * 4 + dz * 2 + dc
            go(remote(s1.at[i], gx.at[x, j, own_rows], d_send, d_recv.at[j], dev_dp(dy, dz, dc)))

    def d_wait(i):
        remote(s1.at[i], gx.at[x, i, own_rows], d_send, d_recv.at[i], dev_dp(0, 0, 1)).wait_recv()

    def rows_of(start, size, kind):
        if kind < 2:
            return pl.ds(pl.multiple_of(start, 16), size)
        return pl.ds(pl.multiple_of(start + (kind - 2) * (size // 2), 16), size // 2)

    def z_piece(i, step, kind):
        if i in DIRECT:
            kind = 0
        rows = rows_of(at_z(step) * ZROWS, ZROWS, kind)
        return gx.at[:, i, rows] if i in X_FIRST else gx.at[x, i, rows]

    def x_piece(i, step, kind):
        rows = rows_of(zh * ZROWS, ZROWS, kind) if i in X_FIRST else rows_of(0, ROWS, kind)
        return gx.at[at_x(step), i, rows]

    def z_ring(i, kind, arriving):
        if i in DIRECT:
            held = (-1, 1, 2)[kind] if arriving else 0
            step = (1, -1, 2)[kind]
        else:
            held = (-1, 1, 2, 2)[kind] if arriving else (0, 0, -1, 1)[kind]
            step = (1, -1, 1, -1)[kind]
        part = z_piece(i, held, kind)
        return remote(part, part, z_send.at[0 if i in X_FIRST else 1], z_recv.at[kind, i], dev_z(step))

    def x_ring(i, kind, arriving):
        held = (-1, 1, 2, 2)[kind] if arriving else (0, 0, -1, 1)[kind]
        step = (1, -1, 1, -1)[kind]
        part = x_piece(i, held, kind)
        return remote(part, part, x_send.at[0 if i in X_FIRST else 1], x_recv.at[kind, i], dev_x(step))

    def add_block(xb, i):
        total = None
        for s in range(SLOTS):
            rows = slice(s * SLOT_LEN, (s + 1) * SLOT_LEN)
            gradient = jnp.dot(att[i, :, rows], gx[xb, i, rows, :], preferred_element_type=jnp.float32)
            square = gradient * gradient
            total = square if total is None else total + square
        acc[xb] += total

    def add_blocks(i, first, count):
        def body(n, carry):
            add_block((x + first + n) % NX, i)
            return carry

        lax.fori_loop(0, count, body, 0)

    waited = set()

    def need(kind, *at):
        if (kind, at) in waited:
            return
        waited.add((kind, at))
        if kind == "d":
            d_wait(*at)
        elif kind == "z":
            z_ring(*at, True).wait_recv()
        elif kind == "x":
            x_ring(*at, True).wait_recv()
        elif kind == "a":
            a_wait(*at)
        else:
            b_copy(*at).wait_recv()

    def need_z(i):
        for kind in range(3 if i in DIRECT else 4):
            need("z", i, kind)

    def need_a(q):
        if q > 0:
            need("a", q)

    def need_d(i):
        if i > 0:
            need("d", i)

    def step(kind, i):
        if kind == "P":
            dp_part(i)
        elif kind == "T":
            attend(i)
        elif kind == "Az":
            go(a_copy(0, 1, 0, 0, 1))
        elif kind == "Ay":
            need_a(i)
            go(a_copy(i, 6 + i, 1 + 3 * i, 1, 0))
            go(a_copy(i, 2 + i, 2 + 3 * i, 3, 0))
        elif kind == "Ao":
            need_a(i)
            go(a_copy(i, 4 + i, 3 + 3 * i, 2, 0))
        elif kind == "A":
            need_a(i)
            go(b_copy(i))
        elif kind == "zo":
            if i in X_FIRST:
                for part in range(4):
                    need("x", i, part)
            else:
                need_d(i)
            for part in range(3 if i in DIRECT else 2):
                go(z_ring(i, part, False))
        elif kind == "zp":
            for part in range(2):
                need("z", i, part)
            for part in (2, 3):
                go(z_ring(i, part, False))
        elif kind == "xo":
            if i in X_FIRST:
                need_d(i)
            else:
                need_z(i)
            for part in range(2):
                go(x_ring(i, part, False))
        elif kind == "xp":
            for part in range(2):
                need("x", i, part)
            for part in (2, 3):
                go(x_ring(i, part, False))
        else:
            if i % 2:
                need("b", i // 2)
            if kind == "c4":
                need_z(i)
                add_blocks(i, 0, 4)
            elif kind == "c3":
                need("x", i, 0)
                need("x", i, 1)
                add_blocks(i, 3, 3)
            else:
                need("x", i, 2)
                need("x", i, 3)
                add_blocks(i, 2, 1)

    for kind, i in ORDER:
        step(kind, i)

    for xb in range(NX):
        out_ref[xb * WIDTH : (xb + 1) * WIDTH, :] = acc[xb].T * (1.0 / (GROUPS * ROWS))

    nx, nz = len(X_FIRST), GROUPS - len(X_FIRST)
    for sem, ref in (
        (x0_send, pk.at[0:3]),
        (d_send, s1.at[1:GROUPS]),
        (a_send, att.at[0:7]),
        (b_send, att.at[0:8]),
        (x_send.at[0], gx.at[0:3, 0:nx, 0:ZROWS]),
        (x_send.at[1], gx.at[0:3, 0:nz]),
        (z_send.at[0], gx.at[0:3, 0:nx]),
        (z_send.at[1], gx.at[0:3, 0:nz, 0:ZROWS]),
    ):
        remote(ref, ref, sem, d_recv.at[0], dev_x(1)).wait_send()


def local(query, keys, values, out_grad, lengths, order):
    vmem = pl.BlockSpec(memory_space=pltpu.VMEM)
    hbm = pl.BlockSpec(memory_space=pl.ANY)
    bf16 = jnp.bfloat16
    dma = pltpu.SemaphoreType.DMA
    summed = pl.pallas_call(
        kernel,
        out_shape=jax.ShapeDtypeStruct((NX * WIDTH, FEATS), jnp.float32),
        in_specs=[hbm] * 6,
        out_specs=vmem,
        scratch_shapes=[
            pltpu.SMEM(lengths.shape, jnp.int32),
            pltpu.SMEM(order.shape, jnp.int32),
            pltpu.VMEM(query.shape, bf16),
            pltpu.VMEM(out_grad.shape, bf16),
            pltpu.VMEM((ROWS, HEAD_DIM), bf16),
            pltpu.VMEM((ROWS, HEAD_DIM), bf16),
            pltpu.VMEM((NX, GROUPS * PIECE, WIDTH), bf16),
            pltpu.VMEM((NX, GROUPS * PIECE, WIDTH), bf16),
            pltpu.VMEM((GROUPS, ZROWS, WIDTH), bf16),
            pltpu.VMEM((NX, GROUPS, ROWS, WIDTH), bf16),
            pltpu.VMEM((GROUPS, FEATS, ROWS), bf16),
            pltpu.VMEM((NX, FEATS, WIDTH), jnp.float32),
            dma((6,)),
            dma, dma((3, NY)),
            dma, dma((GROUPS,)),
            dma((2,)), dma((4, GROUPS)),
            dma((2,)), dma((4, GROUPS)),
            dma, dma((8,)),
            dma, dma((8,)),
        ],
        compiler_params=pltpu.CompilerParams(
            collective_id=0, has_side_effects=True, vmem_limit_bytes=60 * 1024 * 1024
        ),
        cost_estimate=pl.CostEstimate(
            flops=2 * 48 * 128 * 512 * 512, bytes_accessed=4 * 1024 * 1024, transcendentals=12 * 128 * 128
        ),
    )(lengths, order, query, keys, values, out_grad)
    return summed


def solution(mesh):
    placed = (P("dp", "tensor"), P("dp", None), P("dp", None), P(("dp", "tensor"), None), P(), P())
    return jax.shard_map(
        local, mesh=mesh, in_specs=placed, out_specs=P("dp", "tensor"), check_vma=False
    )
```

```python
import math

import jax
import jax.numpy as jnp
from jax import lax
from jax.experimental import pallas as pl
from jax.experimental.pallas import tpu as pltpu
from jax.sharding import PartitionSpec as P

HEADS = 64
KV_HEADS = 8
HEAD_DIM = 128
SLOT_LEN = 128
SLOTS = 3
NEGATIVE_FILL = -1e30

NX = 4
NZ = 4
NY = 4
GROUPS = 16
ROWS = SLOTS * SLOT_LEN
PIECE = 24
ZROWS = NX * PIECE
WIDTH = 128
FEATS = 512
PARTS = (0, 2, 1, 3)
X_FIRST = (0, 1, 2)
DIRECT = ()
ORDER = (
    ("T", 0), ("T", 1), ("T", 2), ("P", 0), ("P", 2), ("P", 1), ("P", 3), ("xo", 0),
    ("xo", 1), ("Ay", 0), ("A", 0), ("xo", 2), ("zo", 3), ("zo", 8), ("zo", 12), ("zo", 4),
    ("xp", 0), ("xp", 1), ("xp", 2), ("zp", 3), ("zo", 5), ("zp", 8), ("zo", 6), ("Az", 0),
    ("zp", 12), ("zo", 7), ("zp", 4), ("zo", 9), ("xo", 3), ("zp", 5), ("zo", 10), ("xo", 8),
    ("Az", 1), ("zp", 6), ("zo", 11), ("A", 6), ("A", 2), ("Ap", 0), ("xp", 3), ("xo", 12),
    ("zp", 7), ("zo", 13), ("Az", 2), ("xo", 4), ("xp", 8), ("zp", 9), ("zo", 14), ("xo", 5),
    ("zp", 10), ("zo", 15), ("Ap", 1), ("xp", 12), ("c3", 12), ("Az", 3), ("xo", 6), ("A", 4),
    ("xp", 4), ("c3", 4), ("zp", 11), ("xo", 7), ("zo", 0), ("zp", 13), ("zo", 1), ("c3", 8),
    ("xp", 5), ("Ap", 2), ("c3", 5), ("xo", 9), ("c1", 8), ("c1", 12), ("zp", 14), ("zo", 2),
    ("xp", 6), ("xo", 10), ("zp", 15), ("c1", 4), ("Ap", 3), ("xp", 7), ("xo", 11), ("A", 1),
    ("c1", 5), ("xp", 9), ("c3", 9), ("zp", 0), ("c3", 3), ("xo", 13), ("A", 3), ("A", 7),
    ("c1", 3), ("xp", 10), ("A", 5), ("c3", 6), ("zp", 1), ("xp", 11), ("xo", 14), ("c1", 6),
    ("c3", 7), ("c1", 7), ("c1", 9), ("c3", 10), ("xp", 13), ("c3", 11), ("zp", 2), ("xo", 15),
    ("c1", 10), ("c1", 11), ("c3", 13), ("c4", 0), ("xp", 14), ("c1", 13), ("c3", 14), ("c4", 1),
    ("xp", 15), ("c3", 15), ("c1", 14), ("c4", 2), ("c1", 15),
)
MESH = pl.DeviceIdType.MESH


def kernel(
    lengths_hbm, order_hbm, q_hbm, k_hbm, v_hbm, g_hbm, out_ref,
    lengths_ref, order_ref, q_ref, g_ref, kbuf, vbuf, pk, r0, s1, gx, att, acc,
    kv_sem, x0_send, x0_recv, d_send, d_recv, z_send, z_recv, x_send, x_recv,
    a_send, a_recv, b_send, b_recv,
):
    d = lax.axis_index("dp")
    t = lax.axis_index("tensor")
    zh, x = t // NX, t % NX
    y, zl, c = d // 4, (d // 2) % 2, d % 2

    def at_x(step):
        return (x + step + NX) % NX

    def at_z(step):
        return (zh + step + NZ) % NZ

    def dp_of(dy, dz, dc):
        return ((y + dy) % NY) * 4 + ((zl + dz) % 2) * 2 + (c + dc) % 2

    def dev_x(step):
        return {"dp": d, "tensor": zh * NX + at_x(step)}

    def dev_z(step):
        return {"dp": d, "tensor": at_z(step) * NX + x}

    def dev_dp(dy, dz, dc):
        return {"dp": dp_of(dy, dz, dc), "tensor": t}

    def remote(src, dst, send, recv, device):
        return pltpu.make_async_remote_copy(
            src_ref=src, dst_ref=dst, send_sem=send, recv_sem=recv,
            device_id=device, device_id_type=MESH,
        )

    barrier = pltpu.get_barrier_semaphore()
    peers = [dev_x(s) for s in (1, 2, 3)] + [dev_z(s) for s in (1, 2, 3)]
    peers += [dev_dp(i // 4, (i // 2) % 2, i % 2) for i in range(1, GROUPS)]
    for peer in peers:
        pl.semaphore_signal(barrier, inc=1, device_id=peer, device_id_type=MESH)

    g_copy = pltpu.make_async_copy(g_hbm, g_ref, kv_sem.at[2])
    q_copy = pltpu.make_async_copy(q_hbm, q_ref, kv_sem.at[3])
    l_copy = pltpu.make_async_copy(lengths_hbm, lengths_ref, kv_sem.at[4])
    o_copy = pltpu.make_async_copy(order_hbm, order_ref, kv_sem.at[5])
    g_copy.start()
    kv_cols = pl.ds(pl.multiple_of((t // 2) * HEAD_DIM, HEAD_DIM), HEAD_DIM)
    k_copy = pltpu.make_async_copy(k_hbm.at[:, kv_cols], kbuf, kv_sem.at[0])
    v_copy = pltpu.make_async_copy(v_hbm.at[:, kv_cols], vbuf, kv_sem.at[1])
    k_copy.start()
    q_copy.start()
    v_copy.start()
    l_copy.start()
    o_copy.start()
    g_copy.wait()

    for i in range(0, GROUPS, 2):
        lanes = [dp_of(j // 4, (j // 2) % 2, j % 2) * FEATS for j in (i, i + 1)]
        for xb in range(NX):
            parts = []
            for lane in lanes:
                cols = pl.ds(pl.multiple_of(lane + xb * WIDTH, WIDTH), WIDTH)
                parts.append(g_ref[:, cols].astype(jnp.float32))
            both = jnp.concatenate(parts, axis=0)
            pk[xb, i * PIECE : (i + 2) * PIECE, :] = both.astype(jnp.bfloat16)

    pl.semaphore_wait(barrier, len(peers))

    def go(copy):
        copy.start()

    def x0_rows(dy):
        return pl.ds(dy * 4 * PIECE, 4 * PIECE)

    def x0_start(dy):
        for s in (1, 2, 3):
            go(remote(
                pk.at[at_x(s), x0_rows(dy)], r0.at[x, x0_rows(dy)],
                x0_send, x0_recv.at[s - 1, dy], dev_x(s),
            ))

    for dy in PARTS:
        x0_start(dy)
    r0[x] = pk[x]
    acc[...] = jnp.zeros_like(acc)
    k_copy.wait()
    v_copy.wait()
    q_copy.wait()
    l_copy.wait()
    o_copy.wait()

    key_index = lax.broadcasted_iota(jnp.int32, (SLOT_LEN, SLOT_LEN), 0)
    row_index = lax.broadcasted_iota(jnp.int32, (SLOT_LEN, SLOT_LEN), 1)
    scale = 1.0 / math.sqrt(HEAD_DIM)
    def attend(s):
        length = lengths_ref[order_ref[d * SLOTS + s]]
        rows = slice(s * SLOT_LEN, (s + 1) * SLOT_LEN)
        allowed = (key_index <= row_index) & (key_index < length)
        live = row_index < length
        keys = kbuf[rows, :]
        values_t = vbuf[rows, :].astype(jnp.float32).T.astype(jnp.bfloat16)
        for h in range(FEATS // HEAD_DIM):
            feats = slice(h * HEAD_DIM, (h + 1) * HEAD_DIM)
            scores = lax.dot_general(
                keys, q_ref[rows, feats], (((1,), (1,)), ((), ())),
                preferred_element_type=jnp.float32,
            ) * scale
            scores = jnp.where(allowed, scores, NEGATIVE_FILL)
            peak = jnp.max(scores, axis=0, keepdims=True)
            raised = jnp.exp(scores - peak)
            probs = (raised / jnp.sum(raised, axis=0, keepdims=True)).astype(jnp.bfloat16)
            mixed = jnp.dot(values_t, probs, preferred_element_type=jnp.float32)
            att[0, feats, rows] = jnp.where(live, mixed, 0.0).astype(jnp.bfloat16)

    def a_copy(src, dst, dy, dz, head=None):
        part = slice(0, FEATS) if head is None else slice(head * HEAD_DIM, (head + 1) * HEAD_DIM)
        return remote(
            att.at[2 * src, part], att.at[2 * dst, part], a_send, a_recv.at[dst, head or 0], dev_dp(dy, dz, 0)
        )

    def b_copy(q):
        return remote(att.at[2 * q], att.at[2 * q + 1], b_send, b_recv.at[q], dev_dp(0, 0, 1))

    def a_wait(q):
        for head in range(FEATS // HEAD_DIM) if q % 2 else (None,):
            if q > 1:
                a_copy(q, q, 0, 1, head).wait_recv()

    own_rows = pl.ds(pl.multiple_of(zh * ZROWS, ZROWS), ZROWS)

    def dp_part(dy):
        for s in (1, 2, 3):
            remote(
                pk.at[x, x0_rows(dy)], r0.at[at_x(-s), x0_rows(dy)],
                x0_send, x0_recv.at[s - 1, dy], dev_x(s),
            ).wait_recv()
        for i in range(dy * 4, dy * 4 + 4, 2):
            parts = [r0[xb, i * PIECE : (i + 2) * PIECE, :].astype(jnp.float32) for xb in range(NX)]
            for e in range(2):
                rows = jnp.concatenate([p[e * PIECE : (e + 1) * PIECE] for p in parts], axis=0)
                s1[i + e] = rows.astype(jnp.bfloat16)
        for i in range(dy * 4, dy * 4 + 4):
            if i == 0:
                gx[x, 0, own_rows, :] = s1[0]
                continue
            dz, dc = (i // 2) % 2, i % 2
            j = ((NY - dy) % NY) * 4 + dz * 2 + dc
            go(remote(s1.at[i], gx.at[x, j, own_rows], d_send, d_recv.at[j], dev_dp(dy, dz, dc)))

    def d_wait(i):
        remote(s1.at[i], gx.at[x, i, own_rows], d_send, d_recv.at[i], dev_dp(0, 0, 1)).wait_recv()

    def rows_of(start, size, kind):
        if kind < 2:
            return pl.ds(pl.multiple_of(start, 16), size)
        return pl.ds(pl.multiple_of(start + (kind - 2) * (size // 2), 16), size // 2)

    def z_piece(i, step, kind):
        if i in DIRECT:
            kind = 0
        rows = rows_of(at_z(step) * ZROWS, ZROWS, kind)
        return gx.at[:, i, rows] if i in X_FIRST else gx.at[x, i, rows]

    def x_piece(i, step, kind):
        rows = rows_of(zh * ZROWS, ZROWS, kind) if i in X_FIRST else rows_of(0, ROWS, kind)
        return gx.at[at_x(step), i, rows]

    def z_ring(i, kind, arriving):
        if i in DIRECT:
            held = (-1, 1, 2)[kind] if arriving else 0
            step = (1, -1, 2)[kind]
        else:
            held = (-1, 1, 2, 2)[kind] if arriving else (0, 0, -1, 1)[kind]
            step = (1, -1, 1, -1)[kind]
        part = z_piece(i, held, kind)
        return remote(part, part, z_send.at[0 if i in X_FIRST else 1], z_recv.at[kind, i], dev_z(step))

    def x_ring(i, kind, arriving):
        held = (-1, 1, 2, 2)[kind] if arriving else (0, 0, -1, 1)[kind]
        step = (1, -1, 1, -1)[kind]
        part = x_piece(i, held, kind)
        return remote(part, part, x_send.at[0 if i in X_FIRST else 1], x_recv.at[kind, i], dev_x(step))

    def add_block(xb, i):
        total = None
        for s in range(SLOTS):
            rows = slice(s * SLOT_LEN, (s + 1) * SLOT_LEN)
            gradient = jnp.dot(att[i, :, rows], gx[xb, i, rows, :], preferred_element_type=jnp.float32)
            square = gradient * gradient
            total = square if total is None else total + square
        acc[xb] += total

    def add_blocks(i, first, count):
        def body(n, carry):
            add_block((x + first + n) % NX, i)
            return carry

        lax.fori_loop(0, count, body, 0)

    waited = set()

    def need(kind, *at):
        if (kind, at) in waited:
            return
        waited.add((kind, at))
        if kind == "d":
            d_wait(*at)
        elif kind == "z":
            z_ring(*at, True).wait_recv()
        elif kind == "x":
            x_ring(*at, True).wait_recv()
        elif kind == "a":
            a_wait(*at)
        else:
            b_copy(*at).wait_recv()

    def need_z(i):
        for kind in range(3 if i in DIRECT else 4):
            need("z", i, kind)

    def need_a(q):
        if q > 0:
            need("a", q)

    def need_d(i):
        if i > 0:
            need("d", i)

    def step(kind, i):
        if kind == "P":
            dp_part(i)
        elif kind == "T":
            attend(i)
        elif kind == "Az":
            go(a_copy(0, 1, 0, 1, i))
        elif kind == "Ap":
            a_copy(1, 1, 0, 1, i).wait_recv()
            go(a_copy(1, 7, 1, 0, i))
            go(a_copy(1, 3, 3, 0, i))
            go(a_copy(1, 5, 2, 0, i))
        elif kind == "Ay":
            go(a_copy(0, 6, 1, 0))
            go(a_copy(0, 2, 3, 0))
            go(a_copy(0, 4, 2, 0))
        elif kind == "A":
            need_a(i)
            go(b_copy(i))
        elif kind == "zo":
            if i in X_FIRST:
                for part in range(4):
                    need("x", i, part)
            else:
                need_d(i)
            for part in range(3 if i in DIRECT else 2):
                go(z_ring(i, part, False))
        elif kind == "zp":
            for part in range(2):
                need("z", i, part)
            for part in (2, 3):
                go(z_ring(i, part, False))
        elif kind == "xo":
            if i in X_FIRST:
                need_d(i)
            else:
                need_z(i)
            for part in range(2):
                go(x_ring(i, part, False))
        elif kind == "xp":
            for part in range(2):
                need("x", i, part)
            for part in (2, 3):
                go(x_ring(i, part, False))
        else:
            if i % 2:
                need("b", i // 2)
            if kind == "c4":
                need_z(i)
                add_blocks(i, 0, 4)
            elif kind == "c3":
                need("x", i, 0)
                need("x", i, 1)
                add_blocks(i, 3, 3)
            else:
                need("x", i, 2)
                need("x", i, 3)
                add_blocks(i, 2, 1)

    for kind, i in ORDER:
        step(kind, i)

    for xb in range(NX):
        out_ref[xb * WIDTH : (xb + 1) * WIDTH, :] = acc[xb].T * (1.0 / (GROUPS * ROWS))

    nx, nz = len(X_FIRST), GROUPS - len(X_FIRST)
    for sem, ref in (
        (x0_send, pk.at[0:3]),
        (d_send, s1.at[1:GROUPS]),
        (a_send, att.at[0:7]),
        (b_send, att.at[0:8]),
        (x_send.at[0], gx.at[0:3, 0:nx, 0:ZROWS]),
        (x_send.at[1], gx.at[0:3, 0:nz]),
        (z_send.at[0], gx.at[0:3, 0:nx]),
        (z_send.at[1], gx.at[0:3, 0:nz, 0:ZROWS]),
    ):
        remote(ref, ref, sem, d_recv.at[0], dev_x(1)).wait_send()


def local(query, keys, values, out_grad, lengths, order):
    vmem = pl.BlockSpec(memory_space=pltpu.VMEM)
    hbm = pl.BlockSpec(memory_space=pl.ANY)
    bf16 = jnp.bfloat16
    dma = pltpu.SemaphoreType.DMA
    summed = pl.pallas_call(
        kernel,
        out_shape=jax.ShapeDtypeStruct((NX * WIDTH, FEATS), jnp.float32),
        in_specs=[hbm] * 6,
        out_specs=vmem,
        scratch_shapes=[
            pltpu.SMEM(lengths.shape, jnp.int32),
            pltpu.SMEM(order.shape, jnp.int32),
            pltpu.VMEM(query.shape, bf16),
            pltpu.VMEM(out_grad.shape, bf16),
            pltpu.VMEM((ROWS, HEAD_DIM), bf16),
            pltpu.VMEM((ROWS, HEAD_DIM), bf16),
            pltpu.VMEM((NX, GROUPS * PIECE, WIDTH), bf16),
            pltpu.VMEM((NX, GROUPS * PIECE, WIDTH), bf16),
            pltpu.VMEM((GROUPS, ZROWS, WIDTH), bf16),
            pltpu.VMEM((NX, GROUPS, ROWS, WIDTH), bf16),
            pltpu.VMEM((GROUPS, FEATS, ROWS), bf16),
            pltpu.VMEM((NX, FEATS, WIDTH), jnp.float32),
            dma((6,)),
            dma, dma((3, NY)),
            dma, dma((GROUPS,)),
            dma((2,)), dma((4, GROUPS)),
            dma((2,)), dma((4, GROUPS)),
            dma, dma((8, 4)),
            dma, dma((8,)),
        ],
        compiler_params=pltpu.CompilerParams(
            collective_id=0, has_side_effects=True, vmem_limit_bytes=60 * 1024 * 1024
        ),
        cost_estimate=pl.CostEstimate(
            flops=2 * 48 * 128 * 512 * 512, bytes_accessed=4 * 1024 * 1024, transcendentals=12 * 128 * 128
        ),
    )(lengths, order, query, keys, values, out_grad)
    return summed


def solution(mesh):
    placed = (P("dp", "tensor"), P("dp", None), P("dp", None), P(("dp", "tensor"), None), P(), P())
    return jax.shard_map(
        local, mesh=mesh, in_specs=placed, out_specs=P("dp", "tensor"), check_vma=False
    )
```

```python
import math

import jax
import jax.numpy as jnp
from jax import lax
from jax.experimental import pallas as pl
from jax.experimental.pallas import tpu as pltpu
from jax.sharding import PartitionSpec as P

HEADS = 64
KV_HEADS = 8
HEAD_DIM = 128
SLOT_LEN = 128
SLOTS = 3
NEGATIVE_FILL = -1e30

NX = 4
NZ = 4
NY = 4
GROUPS = 16
ROWS = SLOTS * SLOT_LEN
PIECE = 24
ZROWS = NX * PIECE
WIDTH = 128
FEATS = 512
PARTS = (0, 2, 1, 3)
X_FIRST = (0, 1, 2)
DIRECT = ()
ORDER = (
    ("T", 0), ("T", 1), ("T", 2), ("P", 0), ("P", 2), ("P", 1), ("P", 3), ("xo", 0),
    ("xo", 1), ("Ay", 0), ("A", 0), ("xo", 2), ("zo", 3), ("zo", 8), ("zo", 12), ("zo", 4),
    ("xp", 0), ("xp", 1), ("xp", 2), ("zp", 3), ("zo", 5), ("zp", 8), ("zo", 6), ("Az", 0),
    ("zp", 12), ("zo", 7), ("zp", 4), ("zo", 9), ("xo", 3), ("zp", 5), ("zo", 10), ("xo", 8),
    ("Az", 1), ("zp", 6), ("zo", 11), ("A", 6), ("A", 2), ("Ap", 0), ("xp", 3), ("xo", 12),
    ("zp", 7), ("zo", 13), ("Az", 2), ("xo", 4), ("xp", 8), ("zp", 9), ("zo", 14), ("xo", 5),
    ("zp", 10), ("zo", 15), ("Ap", 1), ("xp", 12), ("c3", 12), ("Az", 3), ("xo", 6), ("A", 4),
    ("xp", 4), ("c3", 4), ("zp", 11), ("xo", 7), ("zo", 0), ("zp", 13), ("zo", 1), ("c3", 8),
    ("xp", 5), ("Ap", 2), ("c3", 5), ("xo", 9), ("c1", 8), ("c1", 12), ("zp", 14), ("zo", 2),
    ("xp", 6), ("xo", 10), ("zp", 15), ("c1", 4), ("Ap", 3), ("xp", 7), ("xo", 11), ("A", 1),
    ("c1", 5), ("xp", 9), ("c3", 9), ("zp", 0), ("c3", 3), ("xo", 13), ("A", 3), ("A", 7),
    ("c1", 3), ("xp", 10), ("A", 5), ("c3", 6), ("zp", 1), ("xp", 11), ("xo", 14), ("c1", 6),
    ("c3", 7), ("c1", 7), ("c1", 9), ("c3", 10), ("xp", 13), ("c3", 11), ("zp", 2), ("xo", 15),
    ("c1", 10), ("c1", 11), ("c3", 13), ("c4", 0), ("xp", 14), ("c1", 13), ("c3", 14), ("c4", 1),
    ("xp", 15), ("c3", 15), ("c1", 14), ("c4", 2), ("c1", 15),
)
MESH = pl.DeviceIdType.MESH


def kernel(
    lengths_hbm, order_hbm, q_hbm, k_hbm, v_hbm, g_hbm, out_ref,
    lengths_ref, order_ref, q_ref, g_ref, kbuf, vbuf, pk, r0, s1, gx, att, acc,
    kv_sem, x0_send, x0_recv, d_send, d_recv, z_send, z_recv, x_send, x_recv,
    a_send, a_recv, b_send, b_recv,
):
    d = lax.axis_index("dp")
    t = lax.axis_index("tensor")
    zh, x = t // NX, t % NX
    y, zl, c = d // 4, (d // 2) % 2, d % 2

    def at_x(step):
        return (x + step + NX) % NX

    def at_z(step):
        return (zh + step + NZ) % NZ

    def dp_of(dy, dz, dc):
        return ((y + dy) % NY) * 4 + ((zl + dz) % 2) * 2 + (c + dc) % 2

    def dev_x(step):
        return {"dp": d, "tensor": zh * NX + at_x(step)}

    def dev_z(step):
        return {"dp": d, "tensor": at_z(step) * NX + x}

    def dev_dp(dy, dz, dc):
        return {"dp": dp_of(dy, dz, dc), "tensor": t}

    def remote(src, dst, send, recv, device):
        return pltpu.make_async_remote_copy(
            src_ref=src, dst_ref=dst, send_sem=send, recv_sem=recv,
            device_id=device, device_id_type=MESH,
        )

    barrier = pltpu.get_barrier_semaphore()
    peers = [dev_x(s) for s in (1, 2, 3)] + [dev_z(1), dev_z(-1)]
    peers += [dev_dp(i // 4, (i // 2) % 2, i % 2) for i in range(1, GROUPS)]
    for peer in peers:
        pl.semaphore_signal(barrier, inc=1, device_id=peer, device_id_type=MESH)

    g_copy = pltpu.make_async_copy(g_hbm, g_ref, kv_sem.at[2])
    q_copy = pltpu.make_async_copy(q_hbm, q_ref, kv_sem.at[3])
    l_copy = pltpu.make_async_copy(lengths_hbm, lengths_ref, kv_sem.at[4])
    o_copy = pltpu.make_async_copy(order_hbm, order_ref, kv_sem.at[5])
    g_copy.start()
    kv_cols = pl.ds(pl.multiple_of((t // 2) * HEAD_DIM, HEAD_DIM), HEAD_DIM)
    k_copy = pltpu.make_async_copy(k_hbm.at[:, kv_cols], kbuf, kv_sem.at[0])
    v_copy = pltpu.make_async_copy(v_hbm.at[:, kv_cols], vbuf, kv_sem.at[1])
    k_copy.start()
    q_copy.start()
    v_copy.start()
    l_copy.start()
    o_copy.start()
    g_copy.wait()

    for i in range(0, GROUPS, 2):
        lanes = [dp_of(j // 4, (j // 2) % 2, j % 2) * FEATS for j in (i, i + 1)]
        for xb in range(NX):
            parts = []
            for lane in lanes:
                cols = pl.ds(pl.multiple_of(lane + xb * WIDTH, WIDTH), WIDTH)
                parts.append(g_ref[:, cols].astype(jnp.float32))
            both = jnp.concatenate(parts, axis=0)
            pk[xb, i * PIECE : (i + 2) * PIECE, :] = both.astype(jnp.bfloat16)

    pl.semaphore_wait(barrier, len(peers))

    def go(copy):
        copy.start()

    def x0_rows(dy):
        return pl.ds(dy * 4 * PIECE, 4 * PIECE)

    def x0_start(dy):
        for s in (1, 2, 3):
            go(remote(
                pk.at[at_x(s), x0_rows(dy)], r0.at[x, x0_rows(dy)],
                x0_send, x0_recv.at[s - 1, dy], dev_x(s),
            ))

    for dy in PARTS:
        x0_start(dy)
    r0[x] = pk[x]
    acc[...] = jnp.zeros_like(acc)
    k_copy.wait()
    v_copy.wait()
    q_copy.wait()
    l_copy.wait()
    o_copy.wait()

    key_index = lax.broadcasted_iota(jnp.int32, (SLOT_LEN, SLOT_LEN), 0)
    row_index = lax.broadcasted_iota(jnp.int32, (SLOT_LEN, SLOT_LEN), 1)
    scale = 1.0 / math.sqrt(HEAD_DIM)
    def attend(s):
        length = lengths_ref[order_ref[d * SLOTS + s]]
        rows = slice(s * SLOT_LEN, (s + 1) * SLOT_LEN)
        allowed = (key_index <= row_index) & (key_index < length)
        live = row_index < length
        keys = kbuf[rows, :]
        values_t = vbuf[rows, :].astype(jnp.float32).T.astype(jnp.bfloat16)
        for h in range(FEATS // HEAD_DIM):
            feats = slice(h * HEAD_DIM, (h + 1) * HEAD_DIM)
            scores = lax.dot_general(
                keys, q_ref[rows, feats], (((1,), (1,)), ((), ())),
                preferred_element_type=jnp.float32,
            ) * scale
            scores = jnp.where(allowed, scores, NEGATIVE_FILL)
            peak = jnp.max(scores, axis=0, keepdims=True)
            raised = jnp.exp(scores - peak)
            probs = (raised / jnp.sum(raised, axis=0, keepdims=True)).astype(jnp.bfloat16)
            mixed = jnp.dot(values_t, probs, preferred_element_type=jnp.float32)
            att[0, feats, rows] = jnp.where(live, mixed, 0.0).astype(jnp.bfloat16)

    def a_copy(src, dst, dy, dz, head=None):
        part = slice(0, FEATS) if head is None else slice(head * HEAD_DIM, (head + 1) * HEAD_DIM)
        return remote(
            att.at[2 * src, part], att.at[2 * dst, part], a_send, a_recv.at[dst, head or 0], dev_dp(dy, dz, 0)
        )

    def b_copy(q):
        return remote(att.at[2 * q], att.at[2 * q + 1], b_send, b_recv.at[q], dev_dp(0, 0, 1))

    def a_wait(q):
        for head in range(FEATS // HEAD_DIM) if q % 2 else (None,):
            if q > 1:
                a_copy(q, q, 0, 1, head).wait_recv()

    own_rows = pl.ds(pl.multiple_of(zh * ZROWS, ZROWS), ZROWS)

    def dp_part(dy):
        for s in (1, 2, 3):
            remote(
                pk.at[x, x0_rows(dy)], r0.at[at_x(-s), x0_rows(dy)],
                x0_send, x0_recv.at[s - 1, dy], dev_x(s),
            ).wait_recv()
        for i in range(dy * 4, dy * 4 + 4, 2):
            parts = [r0[xb, i * PIECE : (i + 2) * PIECE, :].astype(jnp.float32) for xb in range(NX)]
            for e in range(2):
                rows = jnp.concatenate([p[e * PIECE : (e + 1) * PIECE] for p in parts], axis=0)
                s1[i + e] = rows.astype(jnp.bfloat16)
        for i in range(dy * 4, dy * 4 + 4):
            if i == 0:
                gx[x, 0, own_rows, :] = s1[0]
                continue
            dz, dc = (i // 2) % 2, i % 2
            j = ((NY - dy) % NY) * 4 + dz * 2 + dc
            go(remote(s1.at[i], gx.at[x, j, own_rows], d_send, d_recv.at[j], dev_dp(dy, dz, dc)))

    def d_wait(i):
        remote(s1.at[i], gx.at[x, i, own_rows], d_send, d_recv.at[i], dev_dp(0, 0, 1)).wait_recv()

    def rows_of(start, size, kind):
        if kind < 2:
            return pl.ds(pl.multiple_of(start, 16), size)
        return pl.ds(pl.multiple_of(start + (kind - 2) * (size // 2), 16), size // 2)

    def z_piece(i, step, kind):
        if i in DIRECT:
            kind = 0
        rows = rows_of(at_z(step) * ZROWS, ZROWS, kind)
        return gx.at[:, i, rows] if i in X_FIRST else gx.at[x, i, rows]

    def x_piece(i, step, kind):
        rows = rows_of(zh * ZROWS, ZROWS, kind) if i in X_FIRST else rows_of(0, ROWS, kind)
        return gx.at[at_x(step), i, rows]

    def z_ring(i, kind, arriving):
        if i in DIRECT:
            held = (-1, 1, 2)[kind] if arriving else 0
            step = (1, -1, 2)[kind]
        else:
            held = (-1, 1, 2, 2)[kind] if arriving else (0, 0, -1, 1)[kind]
            step = (1, -1, 1, -1)[kind]
        part = z_piece(i, held, kind)
        return remote(part, part, z_send.at[0 if i in X_FIRST else 1], z_recv.at[kind, i], dev_z(step))

    def x_ring(i, kind, arriving):
        held = (-1, 1, 2, 2)[kind] if arriving else (0, 0, -1, 1)[kind]
        step = (1, -1, 1, -1)[kind]
        part = x_piece(i, held, kind)
        return remote(part, part, x_send.at[0 if i in X_FIRST else 1], x_recv.at[kind, i], dev_x(step))

    def add_block(xb, i):
        total = None
        for s in range(SLOTS):
            rows = slice(s * SLOT_LEN, (s + 1) * SLOT_LEN)
            gradient = jnp.dot(att[i, :, rows], gx[xb, i, rows, :], preferred_element_type=jnp.float32)
            square = gradient * gradient
            total = square if total is None else total + square
        acc[xb] += total

    def add_pair(xa, xb, i):
        total = None
        for s in range(SLOTS):
            rows = slice(s * SLOT_LEN, (s + 1) * SLOT_LEN)
            grads = jnp.concatenate([gx[xa, i, rows, :], gx[xb, i, rows, :]], axis=1)
            gradient = jnp.dot(att[i, :, rows], grads, preferred_element_type=jnp.float32)
            square = gradient * gradient
            total = square if total is None else total + square
        acc[xa] += total[:, :WIDTH]
        acc[xb] += total[:, WIDTH:]

    def add_blocks(i, first, count):
        if count % 2:
            add_block((x + first) % NX, i)
        for n in range(count % 2, count, 2):
            add_pair((x + first + n) % NX, (x + first + n + 1) % NX, i)

    waited = set()

    def need(kind, *at):
        if (kind, at) in waited:
            return
        waited.add((kind, at))
        if kind == "d":
            d_wait(*at)
        elif kind == "z":
            z_ring(*at, True).wait_recv()
        elif kind == "x":
            x_ring(*at, True).wait_recv()
        elif kind == "a":
            a_wait(*at)
        else:
            b_copy(*at).wait_recv()

    def need_z(i):
        for kind in range(3 if i in DIRECT else 4):
            need("z", i, kind)

    def need_a(q):
        if q > 0:
            need("a", q)

    def need_d(i):
        if i > 0:
            need("d", i)

    def step(kind, i):
        if kind == "P":
            dp_part(i)
        elif kind == "T":
            attend(i)
        elif kind == "Az":
            go(a_copy(0, 1, 0, 1, i))
        elif kind == "Ap":
            a_copy(1, 1, 0, 1, i).wait_recv()
            go(a_copy(1, 7, 1, 0, i))
            go(a_copy(1, 3, 3, 0, i))
            go(a_copy(1, 5, 2, 0, i))
        elif kind == "Ay":
            go(a_copy(0, 6, 1, 0))
            go(a_copy(0, 2, 3, 0))
            go(a_copy(0, 4, 2, 0))
        elif kind == "A":
            need_a(i)
            go(b_copy(i))
        elif kind == "zo":
            if i in X_FIRST:
                for part in range(4):
                    need("x", i, part)
            else:
                need_d(i)
            for part in range(3 if i in DIRECT else 2):
                go(z_ring(i, part, False))
        elif kind == "zp":
            for part in range(2):
                need("z", i, part)
            for part in (2, 3):
                go(z_ring(i, part, False))
        elif kind == "xo":
            if i in X_FIRST:
                need_d(i)
            else:
                need_z(i)
            for part in range(2):
                go(x_ring(i, part, False))
        elif kind == "xp":
            for part in range(2):
                need("x", i, part)
            for part in (2, 3):
                go(x_ring(i, part, False))
        else:
            if i % 2:
                need("b", i // 2)
            if kind == "c4":
                need_z(i)
                add_blocks(i, 0, 4)
            elif kind == "c3":
                need("x", i, 0)
                need("x", i, 1)
                add_blocks(i, 3, 3)
            else:
                need("x", i, 2)
                need("x", i, 3)
                add_blocks(i, 2, 1)

    for kind, i in ORDER:
        step(kind, i)

    for xb in range(NX):
        out_ref[xb * WIDTH : (xb + 1) * WIDTH, :] = acc[xb].T * (1.0 / (GROUPS * ROWS))

    nx, nz = len(X_FIRST), GROUPS - len(X_FIRST)
    for sem, ref in (
        (x0_send, pk.at[0:3]),
        (d_send, s1.at[1:GROUPS]),
        (a_send, att.at[0:7]),
        (b_send, att.at[0:8]),
        (x_send.at[0], gx.at[0:3, 0:nx, 0:ZROWS]),
        (x_send.at[1], gx.at[0:3, 0:nz]),
        (z_send.at[0], gx.at[0:3, 0:nx]),
        (z_send.at[1], gx.at[0:3, 0:nz, 0:ZROWS]),
    ):
        remote(ref, ref, sem, d_recv.at[0], dev_x(1)).wait_send()


def local(query, keys, values, out_grad, lengths, order):
    vmem = pl.BlockSpec(memory_space=pltpu.VMEM)
    hbm = pl.BlockSpec(memory_space=pl.ANY)
    bf16 = jnp.bfloat16
    dma = pltpu.SemaphoreType.DMA
    summed = pl.pallas_call(
        kernel,
        out_shape=jax.ShapeDtypeStruct((NX * WIDTH, FEATS), jnp.float32),
        in_specs=[hbm] * 6,
        out_specs=vmem,
        scratch_shapes=[
            pltpu.SMEM(lengths.shape, jnp.int32),
            pltpu.SMEM(order.shape, jnp.int32),
            pltpu.VMEM(query.shape, bf16),
            pltpu.VMEM(out_grad.shape, bf16),
            pltpu.VMEM((ROWS, HEAD_DIM), bf16),
            pltpu.VMEM((ROWS, HEAD_DIM), bf16),
            pltpu.VMEM((NX, GROUPS * PIECE, WIDTH), bf16),
            pltpu.VMEM((NX, GROUPS * PIECE, WIDTH), bf16),
            pltpu.VMEM((GROUPS, ZROWS, WIDTH), bf16),
            pltpu.VMEM((NX, GROUPS, ROWS, WIDTH), bf16),
            pltpu.VMEM((GROUPS, FEATS, ROWS), bf16),
            pltpu.VMEM((NX, FEATS, WIDTH), jnp.float32),
            dma((6,)),
            dma, dma((3, NY)),
            dma, dma((GROUPS,)),
            dma((2,)), dma((4, GROUPS)),
            dma((2,)), dma((4, GROUPS)),
            dma, dma((8, 4)),
            dma, dma((8,)),
        ],
        compiler_params=pltpu.CompilerParams(
            collective_id=0, has_side_effects=True, vmem_limit_bytes=60 * 1024 * 1024
        ),
        cost_estimate=pl.CostEstimate(
            flops=2 * 48 * 128 * 512 * 512, bytes_accessed=4 * 1024 * 1024, transcendentals=12 * 128 * 128
        ),
    )(lengths, order, query, keys, values, out_grad)
    return summed


def solution(mesh):
    placed = (P("dp", "tensor"), P("dp", None), P("dp", None), P(("dp", "tensor"), None), P(), P())
    return jax.shard_map(
        local, mesh=mesh, in_specs=placed, out_specs=P("dp", "tensor"), check_vma=False
    )
```
